32 devices in a mesh: rows: 16 (over z, y, x), tok: 2 (over core).
Axes of the slice: x: 2, y: 2, z: 4, core: 2. Of those that a mesh axis runs over, the one named last changes fastest.
Arguments:
- calib: bfloat16 [128, 26752], P('tok'), may hold values from -6 to 6
- w_panels: bfloat16 [16384, 256], P(('rows', 'tok')), may hold values from -0.0390625 to 0.0390625
- w_trail: bfloat16 [16384, 26496], P(('rows', 'tok')), may hold values from -0.0390625 to 0.0390625
- keep_mask: int32 [16384, 256], P(('rows', 'tok')), may hold values from 0 to 1, as said below
- factor_block: float32 [256, 256], replicated, as said below
- factor_trail: bfloat16 [256, 26496], P(None, 'rows'), may hold values from -0.359375 to 0.359375
Outputs:
- pruned: bfloat16 [16384, 256], P(('rows', 'tok'))
- next_input: bfloat16 [128, 16384], replicated
The draws below stay inside these ranges and needn't reach their ends.
Inputs may be any that keep to these rules, and one draw needn't show every extreme that they name: `keep_mask`: in every row, each aligned group of 4 columns holds exactly two ones. `factor_block`: upper triangular, diagonal entries between 0.6 and 1.4.
All inputs are finite; a program needn't handle non-finite values.
Results may differ from the reference program's by a relative error of at most 0.001.
Values may be sent and summed in bfloat16 or wider, within the bound.
A program may use at most 192 MiB of HBM per device.

```python
import jax
import jax.numpy as jnp
import numpy as np
from jax import lax

OUT = 16384
PANEL = 128
TRAIL = 26496
TOKENS = 128
COLS = 26752


TWO_OF_FOUR = np.array([[1, 1, 0, 0], [1, 0, 1, 0], [1, 0, 0, 1], [0, 1, 1, 0], [0, 1, 0, 1], [0, 0, 1, 1]], dtype=np.int32)


def draw_keep_mask(key, part):
    pattern_ids = jax.random.randint(key, (OUT, 2 * PANEL // 4), 0, 6)
    pattern_table = jnp.asarray(TWO_OF_FOUR)
    return pattern_table[pattern_ids].reshape(OUT, 2 * PANEL).astype(jnp.int32)


def draw_factor_block(key, part):
    span_total = 2 * PANEL
    key_diag = jax.random.fold_in(key, 11)
    key_upper = jax.random.fold_in(key, 12)
    diagonal = jax.random.uniform(key_diag, (span_total,), jnp.float32, 0.6, 1.4)
    spread = 0.06 * jax.random.normal(key_upper, (span_total, span_total), jnp.float32)
    return (jnp.triu(spread, 1) + jnp.diag(diagonal)).astype(jnp.float32)


def level_of(stream_key, dims, split, least, high):
    def one(axis_at, shards_of):
        heights = jax.random.uniform(jax.random.fold_in(jax.random.fold_in(stream_key, 6), axis_at), (shards_of,), jnp.float32, least / len(split), high / len(split))
        return jnp.repeat(jnp.exp(heights), dims[axis_at] // shards_of).reshape((-1,) + (1,) * (len(dims) - axis_at - 1))

    factor_of = one(*split[0])
    for cut in split[1:]:
        factor_of = factor_of * one(*cut)
    return factor_of


def normal_values(own_key, extent, scale, limit, pieces=(), kind=jnp.bfloat16):
    entries = jax.random.normal(own_key, extent, jnp.float32) * scale
    if len(pieces) > 0:
        entries = level_of(own_key, extent, pieces, -0.22, 0.18) * entries
    return jnp.clip(entries, min=-limit, max=limit).astype(kind)


def setup_inputs(seed: int = 0) -> dict:
    keys = jax.random.split(jax.random.key(seed), 7)
    return {
        "calib": normal_values(keys[0], (TOKENS, COLS), 1.0, 6.0, ((0, 2),)),
        "w_panels": normal_values(keys[1], (OUT, 2 * PANEL), COLS ** -0.5, 0.0390625, ((0, 32),)),
        "w_trail": normal_values(keys[2], (OUT, TRAIL), COLS ** -0.5, 0.0390625, ((0, 32),)),
        "keep_mask": draw_keep_mask(jax.random.fold_in(keys[6], 71), 0),
        "factor_block": draw_factor_block(jax.random.fold_in(keys[6], 71), 0),
        "factor_trail": normal_values(keys[5], (2 * PANEL, TRAIL), 0.06, 0.359375, ((1, 16),)),
    }


def sweep_columns(current, keep_part, factor):
    column_count = factor.shape[0]
    errors = jnp.zeros(current.shape, jnp.float32)
    dropped = 1.0 - keep_part.astype(jnp.float32)

    def advance(column, state_pair):
        weights_now, errors_now = state_pair
        col_index = jnp.asarray(column).astype(jnp.int32)
        values = lax.dynamic_index_in_dim(weights_now, col_index, 1, keepdims=False)
        factor_row = lax.dynamic_index_in_dim(factor, col_index, 0, keepdims=False)
        diag_entry = lax.dynamic_index_in_dim(factor_row, col_index, 0, keepdims=False)
        dropping = lax.dynamic_index_in_dim(dropped, col_index, 1, keepdims=False)
        col_error = dropping * values / diag_entry
        weights_now = weights_now - col_error[:, None] * factor_row[None, :]
        errors_now = lax.dynamic_update_slice_in_dim(errors_now, col_error[:, None], col_index, 1)
        return weights_now, errors_now

    return lax.fori_loop(0, column_count, advance, (current, errors))


def reference(calib, w_panels, w_trail, keep_mask, factor_block, factor_trail):
    span_total = factor_block.shape[0]
    current, errors = sweep_columns(w_panels.astype(jnp.float32), keep_mask, factor_block)
    final_weights = current * keep_mask.astype(jnp.float32)
    pruned = final_weights.astype(jnp.bfloat16)
    x_panel = calib[:, :span_total].astype(jnp.float32)
    x_trail = calib[:, span_total:]
    contract = (((1,), (1,)), ((), ()))
    part_panel = lax.dot_general(x_panel, final_weights, contract, precision=lax.Precision.HIGHEST)
    base_trail = lax.dot_general(x_trail, w_trail, contract, preferred_element_type=jnp.float32)
    projected = lax.dot_general(x_trail, factor_trail, contract, preferred_element_type=jnp.float32)
    part_trail = base_trail - lax.dot_general(projected, errors, contract, precision=lax.Precision.HIGHEST)
    next_input = (part_panel + part_trail).astype(jnp.bfloat16)
    return pruned, next_input
```

```python
import functools

import jax
import jax.numpy as jnp
from jax import lax
from jax.experimental import pallas as pl
from jax.experimental.pallas import tpu as pltpu
from jax.sharding import PartitionSpec as P

F32, BF16 = jnp.float32, jnp.bfloat16
SUPER = 64
NT = (((1,), (1,)), ((), ()))


def split(value):
    high = value.astype(BF16)
    return high, (value - high.astype(F32)).astype(BF16)


def sweep_kernel(w_ref, keep_ref, factor_ref, pruned_ref, sides_ref, cur, scale, errs):
    span = factor_ref.shape[0]
    factor = factor_ref[...]
    on_diag = lax.broadcasted_iota(jnp.int32, factor.shape, 0) == lax.broadcasted_iota(
        jnp.int32, factor.shape, 1
    )
    diagonal = jnp.sum(jnp.where(on_diag, factor, 0.0), axis=1, keepdims=True)
    factor_t = factor.T
    high, low = split(factor_t)
    cur[...] = w_ref[...].astype(F32).T
    dropped = 1.0 - keep_ref[...].astype(F32).T
    scale[...] = dropped / diagonal
    for start in range(0, span, SUPER):
        stop = start + SUPER
        groups = [cur[start + g : start + g + 8, :] for g in range(0, SUPER, 8)]
        for group in range(SUPER // 8):
            base = start + group * 8
            rates = scale[base : base + 8, :]
            rows = []
            for inner in range(8):
                col = base + inner
                row = rates[inner : inner + 1, :] * groups[group][inner : inner + 1, :]
                rows.append(row)
                for g in range(group, SUPER // 8):
                    lead = factor_t[start + g * 8 : start + g * 8 + 8, col : col + 1]
                    groups[g] = groups[g] - lead * row
            errs[base : base + 8, :] = jnp.concatenate(rows, axis=0)
        for g in range(SUPER // 8):
            cur[start + g * 8 : start + g * 8 + 8, :] = groups[g]
        if stop < span:
            err_high, err_low = split(errs[start:stop, :])
            left_high, left_low = high[stop:, start:stop], low[stop:, start:stop]
            dot = functools.partial(jnp.dot, preferred_element_type=F32)
            cur[stop:, :] = cur[stop:, :] - (
                dot(left_high, err_high) + (dot(left_high, err_low) + dot(left_low, err_high))
            )
    final = cur[...] * (1.0 - dropped)
    pruned_ref[...] = final.T.astype(BF16)
    sides_ref[0], sides_ref[1] = split(final)
    sides_ref[2], sides_ref[3] = split(errs[...])


def sweep(w_panels, keep_mask, factor_block):
    rows, span = w_panels.shape
    return pl.pallas_call(
        sweep_kernel,
        out_shape=(
            jax.ShapeDtypeStruct((rows, span), BF16),
            jax.ShapeDtypeStruct((4, span, rows), BF16),
        ),
        scratch_shapes=[pltpu.VMEM((span, rows), F32)] * 3,
        compiler_params=pltpu.CompilerParams(vmem_limit_bytes=32 << 20),
    )(w_panels, keep_mask, factor_block)


def partial_projection(calib, factor_trail, span):
    width = factor_trail.shape[1]
    start = span + lax.axis_index("rows") * width
    own = lax.dynamic_slice_in_dim(calib, start, width, 1)
    return lax.dot_general(own, factor_trail, NT, preferred_element_type=F32)


def simple_device(calib, w_panels, w_trail, keep_mask, factor_block, factor_trail):
    span = factor_block.shape[0]
    tokens = lax.all_gather(calib, "tok", axis=0, tiled=True)
    partial = partial_projection(calib, factor_trail, span)
    projected = lax.all_gather(lax.psum(partial, "rows"), "tok", axis=0, tiled=True)
    pruned, sides = sweep(w_panels, keep_mask, factor_block)
    total = lax.dot_general(tokens[:, span:], w_trail, NT, preferred_element_type=F32)
    dot = functools.partial(jnp.dot, preferred_element_type=F32)
    x_panel = tokens[:, :span]
    high = lax.reduce_precision(projected, 8, 7)
    low = (projected - high).astype(BF16)
    high = high.astype(BF16)
    total = total + (dot(x_panel, sides[0]) + dot(x_panel, sides[1]))
    total = total - (dot(high, sides[2]) + (dot(high, sides[3]) + dot(low, sides[2])))
    local = total.astype(BF16)
    return pruned, lax.all_gather(local, ("rows", "tok"), axis=1, tiled=True)


def solution(mesh):
    placed = (
        P("tok", None),
        P(("rows", "tok"), None),
        P(("rows", "tok"), None),
        P(("rows", "tok"), None),
        P(),
        P(None, "rows"),
    )
    return jax.shard_map(
        simple_device,
        mesh=mesh,
        in_specs=placed,
        out_specs=(P(("rows", "tok"), None), P()),
        check_vma=False,
    )
```

```python
import functools

import jax
import jax.numpy as jnp
from jax import lax
from jax.experimental import pallas as pl
from jax.experimental.pallas import tpu as pltpu
from jax.sharding import PartitionSpec as P

F32, BF16 = jnp.float32, jnp.bfloat16
SUPER = 64
NT = (((1,), (1,)), ((), ()))


def split(value):
    high = value.astype(BF16)
    return high, (value - high.astype(F32)).astype(BF16)


def sweep_kernel(w_ref, keep_ref, factor_ref, pruned_ref, sides_ref, cur, scale, errs):
    span = factor_ref.shape[0]
    factor = factor_ref[...]
    on_diag = lax.broadcasted_iota(jnp.int32, factor.shape, 0) == lax.broadcasted_iota(
        jnp.int32, factor.shape, 1
    )
    diagonal = jnp.sum(jnp.where(on_diag, factor, 0.0), axis=1, keepdims=True)
    factor_t = factor.T
    high, low = split(factor_t)
    cur[...] = w_ref[...].astype(F32).T
    dropped = 1.0 - keep_ref[...].astype(F32).T
    scale[...] = dropped / diagonal
    for start in range(0, span, SUPER):
        stop = start + SUPER
        groups = [cur[start + g : start + g + 8, :] for g in range(0, SUPER, 8)]
        for group in range(SUPER // 8):
            base = start + group * 8
            rates = scale[base : base + 8, :]
            rows = []
            for inner in range(8):
                col = base + inner
                row = rates[inner : inner + 1, :] * groups[group][inner : inner + 1, :]
                rows.append(row)
                for g in range(group, SUPER // 8):
                    lead = factor_t[start + g * 8 : start + g * 8 + 8, col : col + 1]
                    groups[g] = groups[g] - lead * row
            errs[base : base + 8, :] = jnp.concatenate(rows, axis=0)
        for g in range(SUPER // 8):
            cur[start + g * 8 : start + g * 8 + 8, :] = groups[g]
        if stop < span:
            err_high, err_low = split(errs[start:stop, :])
            left_high, left_low = high[stop:, start:stop], low[stop:, start:stop]
            dot = functools.partial(jnp.dot, preferred_element_type=F32)
            cur[stop:, :] = cur[stop:, :] - (
                dot(left_high, err_high) + (dot(left_high, err_low) + dot(left_low, err_high))
            )
    final = cur[...] * (1.0 - dropped)
    pruned_ref[...] = final.T.astype(BF16)
    sides_ref[0], sides_ref[1] = split(final)
    sides_ref[2], sides_ref[3] = split(errs[...])


def sweep(w_panels, keep_mask, factor_block):
    rows, span = w_panels.shape
    return pl.pallas_call(
        sweep_kernel,
        out_shape=(
            jax.ShapeDtypeStruct((rows, span), BF16),
            jax.ShapeDtypeStruct((4, span, rows), BF16),
        ),
        scratch_shapes=[pltpu.VMEM((span, rows), F32)] * 3,
        compiler_params=pltpu.CompilerParams(vmem_limit_bytes=32 << 20),
    )(w_panels, keep_mask, factor_block)


def partial_projection(calib, factor_trail, span):
    width = factor_trail.shape[1]
    start = span + lax.axis_index("rows") * width
    own = lax.dynamic_slice_in_dim(calib, start, width, 1)
    return lax.dot_general(own, factor_trail, NT, preferred_element_type=F32)


def simple_device(calib, w_panels, w_trail, keep_mask, factor_block, factor_trail):
    span = factor_block.shape[0]
    tokens = lax.all_gather(calib, "tok", axis=0, tiled=True)
    partial = partial_projection(calib, factor_trail, span)
    projected = lax.all_gather(lax.psum(partial, "rows"), "tok", axis=0, tiled=True)
    pruned, sides = sweep(w_panels, keep_mask, factor_block)
    total = lax.dot_general(tokens[:, span:], w_trail, NT, preferred_element_type=F32)
    dot = functools.partial(jnp.dot, preferred_element_type=F32)
    x_panel = tokens[:, :span]
    high = lax.reduce_precision(projected, 8, 7)
    low = (projected - high).astype(BF16)
    high = high.astype(BF16)
    total = total + (dot(x_panel, sides[0]) + dot(x_panel, sides[1]))
    total = total - (dot(high, sides[2]) + (dot(high, sides[3]) + dot(low, sides[2])))
    local = total.astype(BF16)
    return pruned, lax.all_gather(local, ("rows", "tok"), axis=1, tiled=True)


def remote(src, dst, send_sem, recv_sem, rows, tok):
    return pltpu.make_async_remote_copy(
        src_ref=src,
        dst_ref=dst,
        send_sem=send_sem,
        recv_sem=recv_sem,
        device_id=(rows, tok),
        device_id_type=pl.DeviceIdType.MESH,
    )


def main_kernel(
    n, calib, partial, sides, w, out,
    x, wbuf, own, parts, tile, proj,
    w_sem, x_sem, own_sem, xs, xr, s1, r1, s2, r2, zs, zr, fs, fr, ss, sr, cs, cr,
):
    r, t = lax.axis_index("rows"), lax.axis_index("tok")
    other = 1 - t
    half, span = calib.shape[0], proj.shape[1]
    chunks, width, wide = wbuf.shape
    my_rows = pl.ds(pl.multiple_of(t * half, half), half)

    def w_copy(k):
        cols = pl.ds(pl.multiple_of(k * wide, 128), wide)
        return pltpu.make_async_copy(w.at[:, cols], wbuf.at[k], w_sem.at[k])

    def x_cols(k):
        return pl.ds(pl.multiple_of(span + k * wide, 128), wide)

    def x_copy(k):
        cols = x_cols(k)
        return remote(calib.at[:, cols], x.at[my_rows, cols], xs.at[k], xr.at[k], r, other)

    def panel_copy():
        cols = pl.ds(0, span)
        return remote(
            calib.at[:, cols], x.at[my_rows, cols], xs.at[chunks], xr.at[chunks], r, other
        )

    def loop(low, high, body):
        lax.fori_loop(low, high, lambda i, c: (body(i), c)[1], 0)

    x_local = pltpu.make_async_copy(calib, x.at[my_rows, :], x_sem)
    x_local.start()
    loop(0, chunks, lambda k: w_copy(k).start())

    barrier = pltpu.get_barrier_semaphore()

    def greet(i):
        peer = lax.rem(2 * r + t + i, 2 * n)
        pl.semaphore_signal(
            barrier,
            inc=1,
            device_id=(peer // 2, lax.rem(peer, 2)),
            device_id_type=pl.DeviceIdType.MESH,
        )

    loop(1, 2 * n, greet)
    pl.semaphore_wait(barrier, 2 * n - 1)

    def tile_at(ref, g, base):
        return ref.at[
            pl.ds(pl.multiple_of(base + 8 * (g // 2), 8), 8),
            pl.ds(pl.multiple_of(128 * lax.rem(g, 2), 128), 128),
        ]

    def share(d):
        g = lax.rem(r + d, n)
        return remote(tile_at(partial, g, 0), parts.at[d], s1.at[d], r1.at[d], g, t)

    def spread(i):
        peer = lax.rem(2 * r + t + i, 2 * n)
        return remote(
            tile, tile_at(proj, r, t * half), s2.at[i], r2.at[i], peer // 2, lax.rem(peer, 2)
        )

    loop(1, n, lambda d: share(d).start())
    loop(0, chunks, lambda k: x_copy(k).start())
    panel_copy().start()
    x_local.wait()

    def add_chunk(k, total):
        w_copy(k).wait()
        x_copy(k).wait_recv()
        return total + lax.dot_general(
            wbuf[k], x[:, x_cols(k)], NT, preferred_element_type=F32
        )

    total = jnp.zeros((width, 2 * half), F32)
    early = chunks // 2
    total = lax.fori_loop(0, early, add_chunk, total)
    loop(1, n, lambda d: share(d).wait_recv())
    mine = tile_at(partial, r, 0)[...]
    for d in range(1, n):
        mine = mine + parts[d]
    tile[...] = mine
    loop(1, 2 * n, lambda i: spread(i).start())
    tile_at(proj, r, t * half)[...] = mine
    total = lax.fori_loop(early, chunks, add_chunk, total)
    panel_copy().wait_recv()
    loop(1, 2 * n, lambda i: spread(i).wait_recv())
    dot = functools.partial(jnp.dot, preferred_element_type=F32)
    x_panel = x[:, :span]
    high, low = split(proj[...])
    result = total.T + (dot(x_panel, sides[0]) + dot(x_panel, sides[1]))
    result = result - (dot(high, sides[2]) + (dot(high, sides[3]) + dot(low, sides[2])))
    own[...] = result.astype(BF16)

    z, y, x_at = r // 4, lax.rem(r // 2, 2), lax.rem(r, 2)
    depth = n // 4
    at_y, at_x = r + 2 - 4 * y, r + 1 - 2 * x_at
    plane = 2 * y + x_at

    def region(h, row):
        cols = pl.ds(pl.multiple_of((2 * row + t) * width, 128), width)
        return out.at[pl.ds(h * half, half), cols]

    def mine_of(h):
        return own.at[pl.ds(h * half, half), :]

    def held(kind, dz):
        return lax.rem(z + depth - dz, depth) * 4 + kind

    def first(h):
        return at_y if h == 0 else at_x

    def second(h):
        return at_x if h == 0 else at_y

    def z_send(h, dz):
        to = lax.rem(z + dz, depth) * 4 + plane
        return remote(mine_of(h), region(h, r), zs.at[h, dz], zr.at[h, dz], to, t)

    def place(h, dz, which):
        kind = plane if which == 0 else lax.rem(first(h), 4)
        return held(kind, dz)

    def f_send(h, dz, src=None):
        spot = region(h, place(h, dz, 0))
        src = spot if src is None else src
        return remote(src, spot, fs.at[h, dz], fr.at[h, dz], first(h), t)

    def s_send(h, dz, which, src=None):
        spot = region(h, place(h, dz, which))
        src = spot if src is None else src
        i = which * depth + dz
        return remote(src, spot, ss.at[h, i], sr.at[h, i], second(h), t)

    def c_send(h, i, row, src=None):
        spot = region(h, row)
        src = spot if src is None else src
        return remote(src, spot, cs.at[h, i], cr.at[h, i], r, other)

    local = pltpu.make_async_copy(
        own, out.at[:, pl.ds(pl.multiple_of((2 * r + t) * width, 128), width)], own_sem
    )
    for h in (0, 1):
        f_send(h, 0, mine_of(h)).start()
        s_send(h, 0, 0, mine_of(h)).start()
        loop(1, depth, lambda dz: z_send(h, dz).start())
        c_send(h, 0, r, mine_of(h)).start()
    local.start()

    def from_z(dz):
        for h in (0, 1):
            z_send(h, dz).wait_recv()
            f_send(h, dz).start()
            s_send(h, dz, 0).start()
            c_send(h, dz, place(h, dz, 0)).start()

    loop(1, depth, from_z)

    def from_first(dz):
        for h in (0, 1):
            f_send(h, dz).wait_recv()
            s_send(h, dz, 1).start()
            c_send(h, depth + dz, place(h, dz, 1)).start()

    loop(0, depth, from_first)

    def from_second(dz):
        for h in (0, 1):
            for which in (0, 1):
                s_send(h, dz, which).wait_recv()
                kind = lax.rem(second(h), 4) if which == 0 else 3 - plane
                c_send(h, (2 + which) * depth + dz, held(kind, dz)).start()

    loop(0, depth, from_second)

    def settle_c(i):
        for h in (0, 1):
            c_send(h, i, r).wait()

    loop(0, 4 * depth, settle_c)
    local.wait()

    def settle(dz):
        for h in (0, 1):
            f_send(h, dz).wait_send()
            s_send(h, dz, 0).wait_send()
            s_send(h, dz, 1).wait_send()

    loop(0, depth, settle)

    def settle_z(dz):
        for h in (0, 1):
            z_send(h, dz).wait_send()

    loop(1, depth, settle_z)
    loop(1, n, lambda d: share(d).wait_send())
    loop(1, 2 * n, lambda i: spread(i).wait_send())
    loop(0, chunks, lambda k: x_copy(k).wait_send())
    panel_copy().wait_send()


def main_call(n, calib, partial, sides, w):
    half, cols = calib.shape
    width, trail = w.shape
    span = cols - trail
    tiles = trail // 128
    chunks = next(d for d in range(8, tiles + 1) if tiles % d == 0)
    depth = n // 4
    dma = pltpu.SemaphoreType.DMA
    vmem, anywhere = pl.BlockSpec(memory_space=pltpu.VMEM), pl.BlockSpec(memory_space=pl.ANY)
    return pl.pallas_call(
        functools.partial(main_kernel, n),
        out_shape=jax.ShapeDtypeStruct((2 * half, 2 * n * width), BF16),
        in_specs=[anywhere, vmem, vmem, anywhere],
        out_specs=anywhere,
        scratch_shapes=[
            pltpu.VMEM((2 * half, cols), BF16),
            pltpu.VMEM((chunks, width, trail // chunks), BF16),
            pltpu.VMEM((2 * half, width), BF16),
            pltpu.VMEM((n, 8, 128), F32),
            pltpu.VMEM((8, 128), F32),
            pltpu.VMEM((2 * half, span), F32),
            dma((chunks,)),
            dma,
            dma,
            dma((chunks + 1,)),
            dma((chunks + 1,)),
            dma((n,)),
            dma((n,)),
            dma((2 * n,)),
            dma((2 * n,)),
            dma((2, depth)),
            dma((2, depth)),
            dma((2, depth)),
            dma((2, depth)),
            dma((2, 2 * depth)),
            dma((2, 2 * depth)),
            dma((2, 4 * depth)),
            dma((2, 4 * depth)),
        ],
        compiler_params=pltpu.CompilerParams(
            collective_id=0, has_side_effects=True, vmem_limit_bytes=56 << 20
        ),
    )(calib, partial, sides, w)


def kernel_device(n, calib, w_panels, w_trail, keep_mask, factor_block, factor_trail):
    span = factor_block.shape[0]
    partial = partial_projection(calib, factor_trail, span)
    pruned, sides = sweep(w_panels, keep_mask, factor_block)
    return pruned, main_call(n, calib, partial, sides, w_trail)


def solution(mesh):
    placed = (
        P("tok", None),
        P(("rows", "tok"), None),
        P(("rows", "tok"), None),
        P(("rows", "tok"), None),
        P(),
        P(None, "rows"),
    )
    n = mesh.shape["rows"]

    def per_device(calib, w_panels, *rest):
        half, span, width = calib.shape[0], w_panels.shape[1], w_panels.shape[0]
        fits = half * span == n * 1024 and span == 256 and width % 128 == 0 and n % 4 == 0
        run = functools.partial(kernel_device, n) if fits else simple_device
        return run(calib, w_panels, *rest)

    return jax.shard_map(
        per_device,
        mesh=mesh,
        in_specs=placed,
        out_specs=(P(("rows", "tok"), None), P()),
        check_vma=False,
    )
```

```python
import functools

import jax
import jax.numpy as jnp
from jax import lax
from jax.experimental import pallas as pl
from jax.experimental.pallas import tpu as pltpu
from jax.sharding import PartitionSpec as P

F32, BF16 = jnp.float32, jnp.bfloat16
SUPER = 64
NT = (((1,), (1,)), ((), ()))


def split(value):
    high = value.astype(BF16)
    return high, (value - high.astype(F32)).astype(BF16)


def sweep_kernel(w_ref, keep_ref, factor_ref, pruned_ref, sides_ref, cur, scale, errs):
    span = factor_ref.shape[0]
    factor = factor_ref[...]
    on_diag = lax.broadcasted_iota(jnp.int32, factor.shape, 0) == lax.broadcasted_iota(
        jnp.int32, factor.shape, 1
    )
    diagonal = jnp.sum(jnp.where(on_diag, factor, 0.0), axis=1, keepdims=True)
    factor_t = factor.T
    high, low = split(factor_t)
    cur[...] = w_ref[...].astype(F32).T
    dropped = 1.0 - keep_ref[...].astype(F32).T
    scale[...] = dropped / diagonal
    for start in range(0, span, SUPER):
        stop = start + SUPER
        groups = [cur[start + g : start + g + 8, :] for g in range(0, SUPER, 8)]
        for group in range(SUPER // 8):
            base = start + group * 8
            rates = scale[base : base + 8, :]
            rows = []
            for inner in range(8):
                col = base + inner
                row = rates[inner : inner + 1, :] * groups[group][inner : inner + 1, :]
                rows.append(row)
                for g in range(group, SUPER // 8):
                    lead = factor_t[start + g * 8 : start + g * 8 + 8, col : col + 1]
                    groups[g] = groups[g] - lead * row
            errs[base : base + 8, :] = jnp.concatenate(rows, axis=0)
        for g in range(SUPER // 8):
            cur[start + g * 8 : start + g * 8 + 8, :] = groups[g]
        if stop < span:
            err_high, err_low = split(errs[start:stop, :])
            left_high, left_low = high[stop:, start:stop], low[stop:, start:stop]
            dot = functools.partial(jnp.dot, preferred_element_type=F32)
            cur[stop:, :] = cur[stop:, :] - (
                dot(left_high, err_high) + (dot(left_high, err_low) + dot(left_low, err_high))
            )
    final = cur[...] * (1.0 - dropped)
    pruned_ref[...] = final.T.astype(BF16)
    sides_ref[0], sides_ref[1] = split(final)
    sides_ref[2], sides_ref[3] = split(errs[...])


def sweep(w_panels, keep_mask, factor_block):
    rows, span = w_panels.shape
    return pl.pallas_call(
        sweep_kernel,
        out_shape=(
            jax.ShapeDtypeStruct((rows, span), BF16),
            pltpu.VMEM((4, span, rows), BF16),
        ),
        scratch_shapes=[pltpu.VMEM((span, rows), F32)] * 3,
        compiler_params=pltpu.CompilerParams(vmem_limit_bytes=60 << 20),
    )(w_panels, keep_mask, factor_block)


def partial_projection(calib, factor_trail, span):
    width = factor_trail.shape[1]
    start = span + lax.axis_index("rows") * width
    own = lax.dynamic_slice_in_dim(calib, start, width, 1)
    return lax.dot_general(own, factor_trail, NT, preferred_element_type=F32)


def simple_device(calib, w_panels, w_trail, keep_mask, factor_block, factor_trail):
    span = factor_block.shape[0]
    tokens = lax.all_gather(calib, "tok", axis=0, tiled=True)
    partial = partial_projection(calib, factor_trail, span)
    projected = lax.all_gather(lax.psum(partial, "rows"), "tok", axis=0, tiled=True)
    pruned, sides = sweep(w_panels, keep_mask, factor_block)
    total = lax.dot_general(tokens[:, span:], w_trail, NT, preferred_element_type=F32)
    dot = functools.partial(jnp.dot, preferred_element_type=F32)
    x_panel = tokens[:, :span]
    high = lax.reduce_precision(projected, 8, 7)
    low = (projected - high).astype(BF16)
    high = high.astype(BF16)
    total = total + (dot(x_panel, sides[0]) + dot(x_panel, sides[1]))
    total = total - (dot(high, sides[2]) + (dot(high, sides[3]) + dot(low, sides[2])))
    local = total.astype(BF16)
    return pruned, lax.all_gather(local, ("rows", "tok"), axis=1, tiled=True)


def remote(src, dst, send_sem, recv_sem, rows, tok):
    return pltpu.make_async_remote_copy(
        src_ref=src,
        dst_ref=dst,
        send_sem=send_sem,
        recv_sem=recv_sem,
        device_id=(rows, tok),
        device_id_type=pl.DeviceIdType.MESH,
    )


def main_kernel(
    n, calib, partial, sides, w, out,
    x, wbuf, own, parts, tile, proj,
    w_sem, x_sem, own_sem, xs, xr, s1, r1, s2, r2, zs, zr, fs, fr, ss, sr, cs, cr,
):
    r, t = lax.axis_index("rows"), lax.axis_index("tok")
    other = 1 - t
    half, span = calib.shape[0], proj.shape[1]
    steps, part, wide = wbuf.shape
    chunks, width = steps // 2, 2 * part
    my_rows = pl.ds(pl.multiple_of(t * half, half), half)

    def w_copy(q, k):
        cols = pl.ds(pl.multiple_of(k * wide, 128), wide)
        i = q * chunks + k
        return pltpu.make_async_copy(
            w.at[pl.ds(q * part, part), cols], wbuf.at[i], w_sem.at[i]
        )

    def x_cols(k):
        return pl.ds(pl.multiple_of(span + k * wide, 128), wide)

    def x_copy(k):
        cols = x_cols(k)
        return remote(calib.at[:, cols], x.at[my_rows, cols], xs.at[k], xr.at[k], r, other)

    def panel_copy():
        cols = pl.ds(0, span)
        return remote(
            calib.at[:, cols], x.at[my_rows, cols], xs.at[chunks], xr.at[chunks], r, other
        )

    def loop(low, high, body):
        lax.fori_loop(low, high, lambda i, c: (body(i), c)[1], 0)

    x_local = pltpu.make_async_copy(calib, x.at[my_rows, :], x_sem)
    x_local.start()
    for q in (0, 1):
        loop(0, chunks, lambda k, q=q: w_copy(q, k).start())

    barrier = pltpu.get_barrier_semaphore()

    def greet(i):
        peer = lax.rem(2 * r + t + i, 2 * n)
        pl.semaphore_signal(
            barrier,
            inc=1,
            device_id=(peer // 2, lax.rem(peer, 2)),
            device_id_type=pl.DeviceIdType.MESH,
        )

    loop(1, 2 * n, greet)
    pl.semaphore_wait(barrier, 2 * n - 1)

    def tile_at(ref, g, base):
        return ref.at[
            pl.ds(pl.multiple_of(base + 8 * (g // 2), 8), 8),
            pl.ds(pl.multiple_of(128 * lax.rem(g, 2), 128), 128),
        ]

    def share(d):
        g = lax.rem(r + d, n)
        return remote(tile_at(partial, g, 0), parts.at[d], s1.at[d], r1.at[d], g, t)

    def spread(i):
        peer = lax.rem(2 * r + t + i, 2 * n)
        return remote(
            tile, tile_at(proj, r, t * half), s2.at[i], r2.at[i], peer // 2, lax.rem(peer, 2)
        )

    loop(1, n, lambda d: share(d).start())
    loop(0, chunks, lambda k: x_copy(k).start())
    panel_copy().start()
    x_local.wait()

    def product(q, low, high, total):
        def add_chunk(k, total):
            w_copy(q, k).wait()
            if q == 0:
                x_copy(k).wait_recv()
            return total + lax.dot_general(
                wbuf[q * chunks + k], x[:, x_cols(k)], NT, preferred_element_type=F32
            )

        return lax.fori_loop(low, high, add_chunk, total)

    def finish(q, total):
        dot = functools.partial(jnp.dot, preferred_element_type=F32)
        mine = pl.ds(q * part, part)
        x_panel = x[:, :span]
        high, low = split(proj[...])
        result = total.T + (dot(x_panel, sides[0, :, mine]) + dot(x_panel, sides[1, :, mine]))
        errs_high = sides[2, :, mine]
        result = result - (
            dot(high, errs_high) + (dot(high, sides[3, :, mine]) + dot(low, errs_high))
        )
        own[:, mine] = result.astype(BF16)

    z, y, x_at = r // 4, lax.rem(r // 2, 2), lax.rem(r, 2)
    depth = n // 4
    at_y, at_x = r + 2 - 4 * y, r + 1 - 2 * x_at
    plane = 2 * y + x_at

    def region(v, row):
        cols = pl.ds(pl.multiple_of((2 * row + t) * width + v // 2 * part, 128), part)
        return out.at[pl.ds(v % 2 * half, half), cols]

    def mine_of(v):
        return own.at[pl.ds(v % 2 * half, half), pl.ds(v // 2 * part, part)]

    def held(kind, dz):
        return lax.rem(z + depth - dz, depth) * 4 + kind

    def first(h):
        return at_y if h % 2 == 0 else at_x

    def second(h):
        return at_x if h % 2 == 0 else at_y

    def z_send(h, dz):
        to = lax.rem(z + dz, depth) * 4 + plane
        return remote(mine_of(h), region(h, r), zs.at[h, dz], zr.at[h, dz], to, t)

    def place(h, dz, which):
        kind = plane if which == 0 else lax.rem(first(h), 4)
        return held(kind, dz)

    def f_send(h, dz, src=None):
        spot = region(h, place(h, dz, 0))
        src = spot if src is None else src
        return remote(src, spot, fs.at[h, dz], fr.at[h, dz], first(h), t)

    def s_send(h, dz, which, src=None):
        spot = region(h, place(h, dz, which))
        src = spot if src is None else src
        i = which * depth + dz
        return remote(src, spot, ss.at[h, i], sr.at[h, i], second(h), t)

    def c_send(h, i, row, src=None):
        spot = region(h, row)
        src = spot if src is None else src
        return remote(src, spot, cs.at[h, i], cr.at[h, i], r, other)

    local = pltpu.make_async_copy(
        own, out.at[:, pl.ds(pl.multiple_of((2 * r + t) * width, 128), width)], own_sem
    )

    def send_own(q):
        for h in (2 * q, 2 * q + 1):
            f_send(h, 0, mine_of(h)).start()
            s_send(h, 0, 0, mine_of(h)).start()
            loop(1, depth, lambda dz, h=h: z_send(h, dz).start())
            c_send(h, 0, r, mine_of(h)).start()

    def from_z(q):
        def body(dz):
            for h in (2 * q, 2 * q + 1):
                z_send(h, dz).wait_recv()
                f_send(h, dz).start()
                s_send(h, dz, 0).start()
                c_send(h, dz, place(h, dz, 0)).start()

        loop(1, depth, body)

    def from_first(q):
        def body(dz):
            for h in (2 * q, 2 * q + 1):
                f_send(h, dz).wait_recv()
                s_send(h, dz, 1).start()
                c_send(h, depth + dz, place(h, dz, 1)).start()

        loop(0, depth, body)

    def from_second(q):
        def body(dz):
            for h in (2 * q, 2 * q + 1):
                for which in (0, 1):
                    s_send(h, dz, which).wait_recv()
                    kind = lax.rem(second(h), 4) if which == 0 else 3 - plane
                    c_send(h, (2 + which) * depth + dz, held(kind, dz)).start()

        loop(0, depth, body)

    zero = jnp.zeros((part, 2 * half), F32)
    early = chunks // 2
    total = product(0, 0, early, zero)
    loop(1, n, lambda d: share(d).wait_recv())
    mine = tile_at(partial, r, 0)[...]
    for d in range(1, n):
        mine = mine + parts[d]
    tile[...] = mine
    loop(1, 2 * n, lambda i: spread(i).start())
    tile_at(proj, r, t * half)[...] = mine
    total = product(0, early, chunks, total)
    panel_copy().wait_recv()
    loop(1, 2 * n, lambda i: spread(i).wait_recv())
    finish(0, total)
    send_own(0)
    late = chunks * 2 // 3
    total = product(1, 0, late, zero)
    from_z(0)
    total = product(1, late, chunks, total)
    finish(1, total)
    send_own(1)
    local.start()
    from_first(0)
    from_z(1)
    from_first(1)
    from_second(0)
    from_second(1)

    def settle_c(i):
        for h in range(4):
            c_send(h, i, r).wait()

    loop(0, 4 * depth, settle_c)
    local.wait()

    def settle(dz):
        for h in range(4):
            f_send(h, dz).wait_send()
            s_send(h, dz, 0).wait_send()
            s_send(h, dz, 1).wait_send()

    loop(0, depth, settle)

    def settle_z(dz):
        for h in range(4):
            z_send(h, dz).wait_send()

    loop(1, depth, settle_z)
    loop(1, n, lambda d: share(d).wait_send())
    loop(1, 2 * n, lambda i: spread(i).wait_send())
    loop(0, chunks, lambda k: x_copy(k).wait_send())
    panel_copy().wait_send()


def main_call(n, calib, partial, sides, w):
    half, cols = calib.shape
    width, trail = w.shape
    span = cols - trail
    tiles = trail // 128
    chunks = next(d for d in range(8, tiles + 1) if tiles % d == 0)
    depth = n // 4
    dma = pltpu.SemaphoreType.DMA
    vmem, anywhere = pl.BlockSpec(memory_space=pltpu.VMEM), pl.BlockSpec(memory_space=pl.ANY)
    return pl.pallas_call(
        functools.partial(main_kernel, n),
        out_shape=pltpu.VMEM((2 * half, 2 * n * width), BF16),
        in_specs=[anywhere, vmem, vmem, anywhere],
        out_specs=vmem,
        scratch_shapes=[
            pltpu.VMEM((2 * half, cols), BF16),
            pltpu.VMEM((2 * chunks, width // 2, trail // chunks), BF16),
            pltpu.VMEM((2 * half, width), BF16),
            pltpu.VMEM((n, 8, 128), F32),
            pltpu.VMEM((8, 128), F32),
            pltpu.VMEM((2 * half, span), F32),
            dma((2 * chunks,)),
            dma,
            dma,
            dma((chunks + 1,)),
            dma((chunks + 1,)),
            dma((n,)),
            dma((n,)),
            dma((2 * n,)),
            dma((2 * n,)),
            dma((4, depth)),
            dma((4, depth)),
            dma((4, depth)),
            dma((4, depth)),
            dma((4, 2 * depth)),
            dma((4, 2 * depth)),
            dma((4, 4 * depth)),
            dma((4, 4 * depth)),
        ],
        compiler_params=pltpu.CompilerParams(
            collective_id=0, has_side_effects=True, vmem_limit_bytes=48 << 20
        ),
    )(calib, partial, sides, w)


def kernel_device(n, calib, w_panels, w_trail, keep_mask, factor_block, factor_trail):
    span = factor_block.shape[0]
    partial = partial_projection(calib, factor_trail, span)
    pruned, sides = sweep(w_panels, keep_mask, factor_block)
    return pruned, main_call(n, calib, partial, sides, w_trail)


def solution(mesh):
    placed = (
        P("tok", None),
        P(("rows", "tok"), None),
        P(("rows", "tok"), None),
        P(("rows", "tok"), None),
        P(),
        P(None, "rows"),
    )
    n = mesh.shape["rows"]

    def per_device(calib, w_panels, *rest):
        half, span, width = calib.shape[0], w_panels.shape[1], w_panels.shape[0]
        fits = half * span == n * 1024 and span == 256 and width % 256 == 0 and n % 4 == 0
        run = functools.partial(kernel_device, n) if fits else simple_device
        return run(calib, w_panels, *rest)

    return jax.shard_map(
        per_device,
        mesh=mesh,
        in_specs=placed,
        out_specs=(P(("rows", "tok"), None), P()),
        check_vma=False,
    )
```

```python
import functools

import jax
import jax.numpy as jnp
from jax import lax
from jax.experimental import pallas as pl
from jax.experimental.pallas import tpu as pltpu
from jax.sharding import PartitionSpec as P

F32, BF16 = jnp.float32, jnp.bfloat16
SUPER = 64
NT = (((1,), (1,)), ((), ()))


def split(value):
    high = value.astype(BF16)
    return high, (value - high.astype(F32)).astype(BF16)


def sweep_kernel(w_ref, keep_ref, factor_ref, pruned_ref, sides_ref, cur, scale, errs):
    span = factor_ref.shape[0]
    factor = factor_ref[...]
    on_diag = lax.broadcasted_iota(jnp.int32, factor.shape, 0) == lax.broadcasted_iota(
        jnp.int32, factor.shape, 1
    )
    diagonal = jnp.sum(jnp.where(on_diag, factor, 0.0), axis=1, keepdims=True)
    factor_t = factor.T
    high, low = split(factor_t)
    cur[...] = w_ref[...].astype(F32).T
    dropped = 1.0 - keep_ref[...].astype(F32).T
    scale[...] = dropped / diagonal
    for start in range(0, span, SUPER):
        stop = start + SUPER
        groups = [cur[start + g : start + g + 8, :] for g in range(0, SUPER, 8)]
        for group in range(SUPER // 8):
            base = start + group * 8
            rates = scale[base : base + 8, :]
            rows = []
            for inner in range(8):
                col = base + inner
                row = rates[inner : inner + 1, :] * groups[group][inner : inner + 1, :]
                rows.append(row)
                for g in range(group, SUPER // 8):
                    lead = factor_t[start + g * 8 : start + g * 8 + 8, col : col + 1]
                    groups[g] = groups[g] - lead * row
            errs[base : base + 8, :] = jnp.concatenate(rows, axis=0)
        for g in range(SUPER // 8):
            cur[start + g * 8 : start + g * 8 + 8, :] = groups[g]
        if stop < span:
            err_high, err_low = split(errs[start:stop, :])
            left_high, left_low = high[stop:, start:stop], low[stop:, start:stop]
            dot = functools.partial(jnp.dot, preferred_element_type=F32)
            cur[stop:, :] = cur[stop:, :] - (
                dot(left_high, err_high) + (dot(left_high, err_low) + dot(left_low, err_high))
            )
    final = cur[...] * (1.0 - dropped)
    pruned_ref[...] = final.T.astype(BF16)
    sides_ref[0], sides_ref[1] = split(final)
    sides_ref[2], sides_ref[3] = split(errs[...])


def sweep(w_panels, keep_mask, factor_block):
    rows, span = w_panels.shape
    return pl.pallas_call(
        sweep_kernel,
        out_shape=(
            jax.ShapeDtypeStruct((rows, span), BF16),
            pltpu.VMEM((4, span, rows), BF16),
        ),
        scratch_shapes=[pltpu.VMEM((span, rows), F32)] * 3,
        compiler_params=pltpu.CompilerParams(vmem_limit_bytes=60 << 20),
    )(w_panels, keep_mask, factor_block)


def partial_projection(calib, factor_trail, span):
    width = factor_trail.shape[1]
    start = span + lax.axis_index("rows") * width
    own = lax.dynamic_slice_in_dim(calib, start, width, 1)
    return lax.dot_general(own, factor_trail, NT, preferred_element_type=F32)


def simple_device(calib, w_panels, w_trail, keep_mask, factor_block, factor_trail):
    span = factor_block.shape[0]
    tokens = lax.all_gather(calib, "tok", axis=0, tiled=True)
    partial = partial_projection(calib, factor_trail, span)
    projected = lax.all_gather(lax.psum(partial, "rows"), "tok", axis=0, tiled=True)
    pruned, sides = sweep(w_panels, keep_mask, factor_block)
    total = lax.dot_general(tokens[:, span:], w_trail, NT, preferred_element_type=F32)
    dot = functools.partial(jnp.dot, preferred_element_type=F32)
    x_panel = tokens[:, :span]
    high = lax.reduce_precision(projected, 8, 7)
    low = (projected - high).astype(BF16)
    high = high.astype(BF16)
    total = total + (dot(x_panel, sides[0]) + dot(x_panel, sides[1]))
    total = total - (dot(high, sides[2]) + (dot(high, sides[3]) + dot(low, sides[2])))
    local = total.astype(BF16)
    return pruned, lax.all_gather(local, ("rows", "tok"), axis=1, tiled=True)


def remote(src, dst, send_sem, recv_sem, rows, tok):
    return pltpu.make_async_remote_copy(
        src_ref=src,
        dst_ref=dst,
        send_sem=send_sem,
        recv_sem=recv_sem,
        device_id=(rows, tok),
        device_id_type=pl.DeviceIdType.MESH,
    )


def main_kernel(
    n, calib, partial, w, w_panels, keep, factor, out, pruned,
    sides, cur, scale, errs, x, wbuf, own, parts, tile, proj,
    w_sem, x_sem, own_sem, xs, xr, s1, r1, s2, r2, zs, zr, fs, fr, ss, sr, cs, cr,
):
    r, t = lax.axis_index("rows"), lax.axis_index("tok")
    other = 1 - t
    half, span = calib.shape[0], proj.shape[1]
    steps, part, wide = wbuf.shape
    chunks, width = steps // 2, 2 * part
    my_rows = pl.ds(pl.multiple_of(t * half, half), half)

    def w_copy(q, k):
        cols = pl.ds(pl.multiple_of(k * wide, 128), wide)
        i = q * chunks + k
        return pltpu.make_async_copy(
            w.at[pl.ds(q * part, part), cols], wbuf.at[i], w_sem.at[i]
        )

    def x_cols(k):
        return pl.ds(pl.multiple_of(span + k * wide, 128), wide)

    def x_copy(k):
        cols = x_cols(k)
        return remote(calib.at[:, cols], x.at[my_rows, cols], xs.at[k], xr.at[k], r, other)

    def panel_copy():
        cols = pl.ds(0, span)
        return remote(
            calib.at[:, cols], x.at[my_rows, cols], xs.at[chunks], xr.at[chunks], r, other
        )

    def loop(low, high, body):
        lax.fori_loop(low, high, lambda i, c: (body(i), c)[1], 0)

    x_local = pltpu.make_async_copy(calib, x.at[my_rows, :], x_sem)
    x_local.start()
    for q in (0, 1):
        loop(0, chunks, lambda k, q=q: w_copy(q, k).start())

    barrier = pltpu.get_barrier_semaphore()

    def greet(i):
        peer = lax.rem(2 * r + t + i, 2 * n)
        pl.semaphore_signal(
            barrier,
            inc=1,
            device_id=(peer // 2, lax.rem(peer, 2)),
            device_id_type=pl.DeviceIdType.MESH,
        )

    loop(1, 2 * n, greet)
    pl.semaphore_wait(barrier, 2 * n - 1)

    def tile_at(ref, g, base):
        return ref.at[
            pl.ds(pl.multiple_of(base + 8 * (g // 2), 8), 8),
            pl.ds(pl.multiple_of(128 * lax.rem(g, 2), 128), 128),
        ]

    def share(d):
        g = lax.rem(r + d, n)
        return remote(tile_at(partial, g, 0), parts.at[d], s1.at[d], r1.at[d], g, t)

    def spread(i):
        peer = lax.rem(2 * r + t + i, 2 * n)
        return remote(
            tile, tile_at(proj, r, t * half), s2.at[i], r2.at[i], peer // 2, lax.rem(peer, 2)
        )

    loop(1, n, lambda d: share(d).start())
    loop(0, chunks, lambda k: x_copy(k).start())
    panel_copy().start()
    sweep_kernel(w_panels, keep, factor, pruned, sides, cur, scale, errs)
    x_local.wait()

    def product(q, low, high, total):
        def add_chunk(k, total):
            w_copy(q, k).wait()
            if q == 0:
                x_copy(k).wait_recv()
            return total + lax.dot_general(
                wbuf[q * chunks + k], x[:, x_cols(k)], NT, preferred_element_type=F32
            )

        return lax.fori_loop(low, high, add_chunk, total)

    def finish(q, total):
        dot = functools.partial(jnp.dot, preferred_element_type=F32)
        mine = pl.ds(q * part, part)
        x_panel = x[:, :span]
        high, low = split(proj[...])
        result = total.T + (dot(x_panel, sides[0, :, mine]) + dot(x_panel, sides[1, :, mine]))
        errs_high = sides[2, :, mine]
        result = result - (
            dot(high, errs_high) + (dot(high, sides[3, :, mine]) + dot(low, errs_high))
        )
        own[:, mine] = result.astype(BF16)

    z, y, x_at = r // 4, lax.rem(r // 2, 2), lax.rem(r, 2)
    depth = n // 4
    at_y, at_x = r + 2 - 4 * y, r + 1 - 2 * x_at
    plane = 2 * y + x_at

    def region(v, row):
        cols = pl.ds(pl.multiple_of((2 * row + t) * width + v // 2 * part, 128), part)
        return out.at[pl.ds(v % 2 * half, half), cols]

    def mine_of(v):
        return own.at[pl.ds(v % 2 * half, half), pl.ds(v // 2 * part, part)]

    def held(kind, dz):
        return lax.rem(z + depth - dz, depth) * 4 + kind

    def first(h):
        return at_y if h % 2 == 0 else at_x

    def second(h):
        return at_x if h % 2 == 0 else at_y

    def z_send(h, dz):
        to = lax.rem(z + dz, depth) * 4 + plane
        return remote(mine_of(h), region(h, r), zs.at[h, dz], zr.at[h, dz], to, t)

    def place(h, dz, which):
        kind = plane if which == 0 else lax.rem(first(h), 4)
        return held(kind, dz)

    def f_send(h, dz, src=None):
        spot = region(h, place(h, dz, 0))
        src = spot if src is None else src
        return remote(src, spot, fs.at[h, dz], fr.at[h, dz], first(h), t)

    def s_send(h, dz, which, src=None):
        spot = region(h, place(h, dz, which))
        src = spot if src is None else src
        i = which * depth + dz
        return remote(src, spot, ss.at[h, i], sr.at[h, i], second(h), t)

    def c_send(h, i, row, src=None):
        spot = region(h, row)
        src = spot if src is None else src
        return remote(src, spot, cs.at[h, i], cr.at[h, i], r, other)

    local = pltpu.make_async_copy(
        own, out.at[:, pl.ds(pl.multiple_of((2 * r + t) * width, 128), width)], own_sem
    )

    def send_own(q):
        for h in (2 * q, 2 * q + 1):
            f_send(h, 0, mine_of(h)).start()
            s_send(h, 0, 0, mine_of(h)).start()
            loop(1, depth, lambda dz, h=h: z_send(h, dz).start())
            c_send(h, 0, r, mine_of(h)).start()

    def from_z(q):
        def body(dz):
            for h in (2 * q, 2 * q + 1):
                z_send(h, dz).wait_recv()
                f_send(h, dz).start()
                s_send(h, dz, 0).start()
                c_send(h, dz, place(h, dz, 0)).start()

        loop(1, depth, body)

    def from_first(q):
        def body(dz):
            for h in (2 * q, 2 * q + 1):
                f_send(h, dz).wait_recv()
                s_send(h, dz, 1).start()
                c_send(h, depth + dz, place(h, dz, 1)).start()

        loop(0, depth, body)

    def from_second(q):
        def body(dz):
            for h in (2 * q, 2 * q + 1):
                for which in (0, 1):
                    s_send(h, dz, which).wait_recv()
                    kind = lax.rem(second(h), 4) if which == 0 else 3 - plane
                    c_send(h, (2 + which) * depth + dz, held(kind, dz)).start()

        loop(0, depth, body)

    zero = jnp.zeros((part, 2 * half), F32)
    early = chunks // 2
    total = product(0, 0, early, zero)
    loop(1, n, lambda d: share(d).wait_recv())
    mine = tile_at(partial, r, 0)[...]
    for d in range(1, n):
        mine = mine + parts[d]
    tile[...] = mine
    loop(1, 2 * n, lambda i: spread(i).start())
    tile_at(proj, r, t * half)[...] = mine
    total = product(0, early, chunks, total)
    panel_copy().wait_recv()
    loop(1, 2 * n, lambda i: spread(i).wait_recv())
    finish(0, total)
    send_own(0)
    late = chunks * 2 // 3
    total = product(1, 0, late, zero)
    from_z(0)
    total = product(1, late, chunks, total)
    finish(1, total)
    send_own(1)
    local.start()
    from_first(0)
    from_z(1)
    from_first(1)
    from_second(0)
    from_second(1)

    def settle_c(i):
        for h in range(4):
            c_send(h, i, r).wait()

    loop(0, 4 * depth, settle_c)
    local.wait()

    def settle(dz):
        for h in range(4):
            f_send(h, dz).wait_send()
            s_send(h, dz, 0).wait_send()
            s_send(h, dz, 1).wait_send()

    loop(0, depth, settle)

    def settle_z(dz):
        for h in range(4):
            z_send(h, dz).wait_send()

    loop(1, depth, settle_z)
    loop(1, n, lambda d: share(d).wait_send())
    loop(1, 2 * n, lambda i: spread(i).wait_send())
    loop(0, chunks, lambda k: x_copy(k).wait_send())
    panel_copy().wait_send()


def main_call(n, calib, partial, w, w_panels, keep, factor):
    half, cols = calib.shape
    width, trail = w.shape
    span = cols - trail
    tiles = trail // 128
    chunks = next(d for d in range(8, tiles + 1) if tiles % d == 0)
    depth = n // 4
    dma = pltpu.SemaphoreType.DMA
    vmem, anywhere = pl.BlockSpec(memory_space=pltpu.VMEM), pl.BlockSpec(memory_space=pl.ANY)
    return pl.pallas_call(
        functools.partial(main_kernel, n),
        out_shape=(
            pltpu.VMEM((2 * half, 2 * n * width), BF16),
            pltpu.VMEM((width, span), BF16),
        ),
        in_specs=[anywhere, vmem, anywhere, vmem, vmem, vmem],
        out_specs=(vmem, vmem),
        scratch_shapes=[
            pltpu.VMEM((4, span, width), BF16),
            *[pltpu.VMEM((span, width), F32)] * 3,
            pltpu.VMEM((2 * half, cols), BF16),
            pltpu.VMEM((2 * chunks, width // 2, trail // chunks), BF16),
            pltpu.VMEM((2 * half, width), BF16),
            pltpu.VMEM((n, 8, 128), F32),
            pltpu.VMEM((8, 128), F32),
            pltpu.VMEM((2 * half, span), F32),
            dma((2 * chunks,)),
            dma,
            dma,
            dma((chunks + 1,)),
            dma((chunks + 1,)),
            dma((n,)),
            dma((n,)),
            dma((2 * n,)),
            dma((2 * n,)),
            dma((4, depth)),
            dma((4, depth)),
            dma((4, depth)),
            dma((4, depth)),
            dma((4, 2 * depth)),
            dma((4, 2 * depth)),
            dma((4, 4 * depth)),
            dma((4, 4 * depth)),
        ],
        compiler_params=pltpu.CompilerParams(
            collective_id=0, has_side_effects=True, vmem_limit_bytes=48 << 20
        ),
    )(calib, partial, w, w_panels, keep, factor)


def kernel_device(n, calib, w_panels, w_trail, keep_mask, factor_block, factor_trail):
    span = factor_block.shape[0]
    partial = partial_projection(calib, factor_trail, span)
    gathered, pruned = main_call(
        n, calib, partial, w_trail, w_panels, keep_mask, factor_block
    )
    return pruned, gathered


def solution(mesh):
    placed = (
        P("tok", None),
        P(("rows", "tok"), None),
        P(("rows", "tok"), None),
        P(("rows", "tok"), None),
        P(),
        P(None, "rows"),
    )
    n = mesh.shape["rows"]

    def per_device(calib, w_panels, *rest):
        half, span, width = calib.shape[0], w_panels.shape[1], w_panels.shape[0]
        fits = half * span == n * 1024 and span == 256 and width % 256 == 0 and n % 4 == 0
        run = functools.partial(kernel_device, n) if fits else simple_device
        return run(calib, w_panels, *rest)

    return jax.shard_map(
        per_device,
        mesh=mesh,
        in_specs=placed,
        out_specs=(P(("rows", "tok"), None), P()),
        check_vma=False,
    )
```
